256 devices in a mesh: shot: 32 (over x, y, core), xline: 8 (over z).
Axes of the slice: x: 4, y: 4, z: 8, core: 2. Of those that a mesh axis runs over, the one named last changes fastest.
Arguments:
- records: bfloat16 [64, 512, 2048], P('shot', 'xline'), may hold values from -2 to 2
- source_trace: int32 [32, 32, 16], replicated, may hold values from 0 to 127
- target_trace: int32 [32, 32, 16], P('shot'), may hold values from 0 to 1
- mirror: int32 [32, 32, 16], P('shot'), may hold values from 0 to 511
- live_slots: int32 [32, 32], P('shot'), may hold values from 4 to 16, as said below
Outputs:
- predicted: float32 [64, 512, 2048], P('shot', 'xline')
The draws below stay inside these ranges and needn't reach their ends.
Inputs may be any that keep to these rules, and one draw needn't show every extreme that they name: live_slots[d, d] = 16 for every owner d, and one owner has 16 live slots from every owner.
All inputs are finite; a program needn't handle non-finite values.
Results may differ from the reference program's by a relative error of at most 0.0064.
Values may be sent and summed in bfloat16 or wider, within the bound.
No kernel may reach another device: no remote copies, remote signals or barrier semaphores. Data moves between devices by JAX's collectives and lax.ppermute only.
A program may use at most 128 MiB of HBM per device.

```python
import math
import jax
import jax.numpy as jnp
from jax import lax

NT = 2048
SHOT_DEV = 2
RX = 64
SLOTS = 16
SHOTS = 64
RECV = 512
N_SHOT = 32


def draw_live_slots(key, part):
    key = jax.random.fold_in(key, 11)
    key_weight, key_raw, key_busy = jax.random.split(key, 3)
    owners = SHOTS // SHOT_DEV
    weights = jax.random.randint(key_weight, (owners, 1), 2, 5)
    rawcount = jax.random.randint(key_raw, (owners, owners), SLOTS // 2, SLOTS + 1)
    busiest = jax.random.randint(key_busy, (), 0, owners)
    row_ids = jnp.arange(owners, dtype=jnp.int32)[:, None]
    col_ids = jnp.arange(owners, dtype=jnp.int32)[None, :]
    filled = (row_ids == col_ids) | (row_ids == busiest)
    return jnp.where(filled, SLOTS, rawcount * weights // 4).astype(jnp.int32)


def plant(result, key, low, high):
    longest = result.shape.index(max(result.shape))
    spots = []
    for shift in (0, 1):
        where = [jax.random.randint(jax.random.fold_in(key, axis), (), 0, length) for axis, length in enumerate(result.shape)]
        where[longest] = (where[longest] + shift) % result.shape[longest]
        spots.append(tuple(where))
    return result.at[spots[0]].set(low).at[spots[1]].set(high)


def shard_levels(key, extent, cuts, low, largest):
    level = 1.0
    for axis_at, shards_of in cuts:
        draws = jax.random.uniform(jax.random.fold_in(jax.random.fold_in(key, 6), axis_at), (shards_of,), jnp.float32, low / len(cuts), largest / len(cuts))
        level = level * jnp.repeat(jnp.exp(draws), extent[axis_at] // shards_of).reshape((-1,) + (1,) * (len(extent) - 1 - axis_at))
    return level


def noise(own_key, dims, scale, limit, cuts=(), kind=jnp.bfloat16):
    values = scale * jax.random.normal(own_key, dims, jnp.float32)
    if cuts:
        values = values * shard_levels(own_key, dims, cuts, -0.22, 0.18)
    return jnp.clip(values, -limit, limit).astype(kind)


def setup_inputs(seed: int = 0) -> dict:
    arg_keys = jax.random.split(jax.random.key(seed), 6)
    return {
        "records": noise(arg_keys[0], (SHOTS, RECV, NT), (NT ** -0.25), 2.0, ((0, 32), (1, 8))),
        "source_trace": plant(jax.random.randint(arg_keys[1], (N_SHOT, N_SHOT, SLOTS), 0, SHOT_DEV * RX), jax.random.fold_in(arg_keys[1], 1), 0, (SHOT_DEV * RX) - 1).astype(jnp.int32),
        "target_trace": plant(jax.random.randint(arg_keys[2], (N_SHOT, N_SHOT, SLOTS), 0, SHOT_DEV), jax.random.fold_in(arg_keys[2], 1), 0, SHOT_DEV - 1).astype(jnp.int32),
        "mirror": plant(jax.random.randint(arg_keys[3], (N_SHOT, N_SHOT, SLOTS), 0, RECV), jax.random.fold_in(arg_keys[3], 1), 0, RECV - 1).astype(jnp.int32),
        "live_slots": draw_live_slots(jax.random.fold_in(arg_keys[5], 71), 0),
    }


def tables(length):
    spectral = length // 2
    times_col = jnp.arange(length, dtype=jnp.int32)[:, None]
    freq_row = jnp.arange(spectral, dtype=jnp.int32)[None, :]
    phases = ((times_col * freq_row) % length).astype(jnp.float32) * (2.0 * math.pi / length)
    cos_part = jnp.cos(phases)
    sin_part = jnp.sin(phases)
    forward_full = jnp.concatenate([cos_part, -sin_part], axis=1)
    weights = jnp.where(freq_row == 0, 1.0, 2.0).astype(jnp.float32) / length
    inverse_full = jnp.concatenate([(cos_part * weights).T, (-sin_part * weights).T], axis=0)
    return forward_full.astype(jnp.bfloat16), inverse_full.astype(jnp.bfloat16)


def complex_product(left, right):
    spectral = left.shape[-1] // 2
    left = left.astype(jnp.float32)
    right = right.astype(jnp.float32)
    left_re, left_im = left[:, :spectral], left[:, spectral:]
    right_re, right_im = right[:, :spectral], right[:, spectral:]
    return jnp.concatenate([left_re * right_re - left_im * right_im, left_re * right_im + left_im * right_re], axis=1)


def reference(records, source_trace, target_trace, mirror, live_slots):
    forward, inverse = tables(NT)
    owners = SHOTS // SHOT_DEV
    xlines = RECV // RX

    def transform(block_rows):
        return jnp.dot(block_rows, forward, preferred_element_type=jnp.float32).astype(jnp.bfloat16)

    spectra = lax.map(transform, records)
    spectra_flat = spectra.reshape(SHOTS * RECV, NT)
    dest_col = jnp.arange(owners, dtype=jnp.int32)[:, None, None]
    source_col = jnp.arange(owners, dtype=jnp.int32)[None, :, None]
    slot_ids = jnp.arange(SLOTS, dtype=jnp.int32)[None, None, :]
    usable = (slot_ids < live_slots[:, :, None]).astype(jnp.float32).reshape(-1)
    src_shot = (source_col * SHOT_DEV + source_trace // RX).reshape(-1)
    r_local = (source_trace % RX).reshape(-1)
    dst_shot = (dest_col * SHOT_DEV + target_trace).reshape(-1)
    a_rows = spectra_flat[(dst_shot * RECV + mirror.reshape(-1)).astype(jnp.int32)]
    summed = jnp.zeros((SHOTS * RECV, NT), jnp.float32)
    for xline_pos in range(xlines):
        receiver = xline_pos * RX + r_local
        b_rows = spectra_flat[(src_shot * RECV + receiver).astype(jnp.int32)]
        product = complex_product(a_rows, b_rows) * usable[:, None]
        summed = summed + jax.ops.segment_sum(product, (dst_shot * RECV + receiver).astype(jnp.int32), num_segments=SHOTS * RECV)
    predicted = jnp.dot(summed.astype(jnp.bfloat16), inverse, preferred_element_type=jnp.float32)
    return predicted.reshape(SHOTS, RECV, NT)
```

```python
import functools
import math

import jax
import jax.numpy as jnp
import numpy as np
from jax import lax
from jax.experimental import pallas as pl
from jax.experimental.pallas import tpu as pltpu
from jax.sharding import PartitionSpec as P

VMEM_LIMIT = 48 * 1024 * 1024
TILE = 256


def forward_table(length):
    spectral = length // 2
    t = np.arange(length, dtype=np.int64)[:, None]
    f = np.arange(spectral, dtype=np.int64)[None, :]
    phase = (t * f % length).astype(np.float64) * (2.0 * math.pi / length)
    return np.concatenate([np.cos(phase), -np.sin(phase)], axis=1).astype(jnp.bfloat16)


def transform_kernel(send_ref, rec_ref, table_ref, spec_ref, out_ref, pick):
    @pl.when(pl.program_id(0) == 0)
    def _():
        rows = lax.broadcasted_iota(jnp.int32, pick.shape, 1)
        pick[...] = (rows == send_ref[...]).astype(jnp.float32).astype(jnp.bfloat16)

    spec = jnp.dot(rec_ref[...], table_ref[...], preferred_element_type=jnp.float32).astype(jnp.bfloat16)
    spec_ref[...] = spec
    out_ref[...] = jnp.dot(pick[...], spec, preferred_element_type=jnp.float32).astype(jnp.bfloat16)


def transform(records, send, table):
    rows, length = records.shape
    entries = send.shape[0]
    whole = lambda j: (0, 0)
    cols = lambda j: (0, j)
    return pl.pallas_call(
        transform_kernel,
        grid=(length // TILE,),
        in_specs=[
            pl.BlockSpec((entries, 1), whole),
            pl.BlockSpec((rows, length), whole),
            pl.BlockSpec((length, TILE), cols),
        ],
        out_specs=[pl.BlockSpec((rows, TILE), cols), pl.BlockSpec((entries, TILE), cols)],
        out_shape=[
            jax.ShapeDtypeStruct((rows, length), jnp.bfloat16),
            jax.ShapeDtypeStruct((entries, length), jnp.bfloat16),
        ],
        scratch_shapes=[pltpu.VMEM((entries, rows), jnp.bfloat16)],
        compiler_params=pltpu.CompilerParams(vmem_limit_bytes=VMEM_LIMIT),
    )(send, records, table)


def predict_kernel(
    a_idx_ref, o_idx_ref, sre_ref, sim_ref, bre_ref, bim_ref, tre_ref, tim_ref, out_ref, pick, put
):
    step = pl.program_id(0)
    f32 = jnp.float32

    @pl.when(step == 0)
    def _():
        rows = lax.broadcasted_iota(jnp.int32, pick.shape, 1)
        pick[...] = (rows == a_idx_ref[...]).astype(f32).astype(jnp.bfloat16)
        dest = lax.broadcasted_iota(jnp.int32, put.shape, 0)
        put[...] = (dest == o_idx_ref[...]).astype(f32).astype(jnp.bfloat16)

    a_re = jnp.dot(pick[...], sre_ref[...], preferred_element_type=f32)
    a_im = jnp.dot(pick[...], sim_ref[...], preferred_element_type=f32)
    b_re = bre_ref[...].astype(f32)
    b_im = bim_ref[...].astype(f32)
    length = out_ref.shape[1]
    freq = lax.broadcasted_iota(jnp.int32, (1, TILE), 1) + step * TILE
    scale = jnp.where(freq == 0, 1.0 / length, 2.0 / length).astype(f32)
    total = None
    for product, table in (
        (a_re * b_re - a_im * b_im, tre_ref),
        (a_re * b_im + a_im * b_re, tim_ref),
    ):
        high = product.astype(jnp.bfloat16)
        low = (product - high.astype(f32)).astype(jnp.bfloat16)
        summed = jnp.dot(put[...], high, preferred_element_type=f32)
        summed += jnp.dot(put[...], low, preferred_element_type=f32)
        summed = (summed * scale).astype(jnp.bfloat16)
        part = lax.dot_general(summed, table[...], (((1,), (1,)), ((), ())), preferred_element_type=f32)
        total = part if total is None else total + part

    @pl.when(step == 0)
    def _():
        out_ref[...] = total

    @pl.when(step > 0)
    def _():
        out_ref[...] += total


def predict(a_idx, o_idx, spectra, received, table, rows):
    entries, length = received.shape
    steps = length // 2 // TILE
    whole = lambda j: (0, 0)
    re = lambda j: (0, j)
    im = lambda j: (0, j + steps)
    pair = lambda r: [pl.BlockSpec((r, TILE), re), pl.BlockSpec((r, TILE), im)]
    return pl.pallas_call(
        predict_kernel,
        grid=(steps,),
        in_specs=[
            pl.BlockSpec((entries, 1), whole),
            pl.BlockSpec((1, entries), whole),
            *pair(spectra.shape[0]),
            *pair(entries),
            *pair(length),
        ],
        out_specs=pl.BlockSpec((rows, length), whole),
        out_shape=jax.ShapeDtypeStruct((rows, length), jnp.float32),
        scratch_shapes=[
            pltpu.VMEM((entries, spectra.shape[0]), jnp.bfloat16),
            pltpu.VMEM((rows, entries), jnp.bfloat16),
        ],
        compiler_params=pltpu.CompilerParams(vmem_limit_bytes=VMEM_LIMIT),
    )(a_idx, o_idx, spectra, spectra, received, received, table, table)


def on_device(table, records, source_trace, target_trace, mirror, live_slots):
    shot_dev, rx_local, length = records.shape
    rows = shot_dev * rx_local
    me = lax.axis_index("shot")
    owners, _, slots = source_trace.shape
    send = lax.dynamic_index_in_dim(source_trace, me, 1, False).reshape(-1, 1)
    spec, outgoing = transform(records.reshape(rows, length), send, table)
    spectra = lax.all_gather(spec, "xline", axis=0, tiled=True)
    received = lax.all_to_all(
        outgoing.reshape(owners, slots, length), "shot", split_axis=0, concat_axis=0, tiled=True
    ).reshape(owners * slots, length)
    targets, mirrors = target_trace[0], mirror[0]
    r_local = lax.dynamic_index_in_dim(source_trace, me, 0, False) % rx_local
    live = jnp.arange(slots, dtype=jnp.int32)[None, :] < live_slots[0][:, None]
    a_idx = (mirrors // rx_local * rows + targets * rx_local + mirrors % rx_local).reshape(-1, 1)
    o_idx = jnp.where(live, targets * rx_local + r_local, -1).reshape(1, -1)
    predicted = predict(a_idx, o_idx, spectra, received, table, rows)
    return predicted.reshape(shot_dev, rx_local, length)


def solution(mesh):
    placed = (
        P("shot", "xline", None),
        P(),
        P("shot", None, None),
        P("shot", None, None),
        P("shot", None),
    )

    def run(*args):
        table = jnp.asarray(forward_table(args[0].shape[-1]))
        return jax.shard_map(
            functools.partial(on_device),
            mesh=mesh,
            in_specs=(P(), *placed),
            out_specs=P("shot", "xline", None),
            check_vma=False,
        )(table, *args)

    return run
```

```python
import functools
import math

import jax
import jax.numpy as jnp
import numpy as np
from jax import lax
from jax.experimental import pallas as pl
from jax.experimental.pallas import tpu as pltpu
from jax.sharding import PartitionSpec as P

PARAMS = pltpu.CompilerParams(vmem_limit_bytes=56 * 1024 * 1024)
VMEM = pl.BlockSpec(memory_space=pltpu.VMEM)
ANY = pl.BlockSpec(memory_space=pl.ANY)
TILE = 256
F32 = jnp.float32
BF16 = jnp.bfloat16
CHUNKS = (48, 32)
ROOM = sum(CHUNKS)


def tables(length):
    quarter = length // 4
    t = np.arange(length, dtype=np.int64)[:, None]
    f = np.arange(quarter, dtype=np.int64)[None, :]
    phase = (t * f % length).astype(np.float64) * (2.0 * math.pi / length)
    cos, sin = np.cos(phase), -np.sin(phase)
    turn = t[:, 0] % 4
    sin[:, 0] = np.array([1.0, -1.0, -1.0, 1.0])[turn]
    forward = np.concatenate([cos, sin], axis=1)
    weight = np.full(2 * quarter, 2.0 / length)
    weight[0] = 1.0 / length
    inverse = (forward * weight).T
    return forward.astype(BF16), inverse.astype(BF16)


def dot(left, right):
    return jnp.dot(left, right, preferred_element_type=F32)


def one_hot(left, right):
    return (left == right).astype(F32).astype(BF16)


def iota(shape, axis):
    return lax.broadcasted_iota(jnp.int32, shape, axis)


def tile_at(j, tile=TILE):
    return slice(j * tile, (j + 1) * tile)


def start(source, target, sem):
    copy = pltpu.make_async_copy(source, target, sem)
    copy.start()
    return copy


def open_kernel(xlines, send_ref, want_ref, dest_ref, rec_hbm, table_hbm, *refs):
    out_hbm, *packed_hbm, spec_hbm, full_ref, fast_ref, put_ref = refs[: 5 + len(CHUNKS)]
    rec, table, spec, out, packed, table_sems, out_sems, packed_sems, sems = refs[5 + len(CHUNKS) :]
    count, length = rec.shape
    quarter = length // 4
    first = start(rec_hbm, rec, sems.at[0])
    half = table.shape[0] // 2
    halves = [pl.ds(i * half, half) for i in range(2)]
    coming = [start(table_hbm.at[h], table.at[h], table_sems.at[i]) for i, h in enumerate(halves)]

    owners, slots = send_ref.shape
    entries = owners * slots
    entry, owner = iota((entries, owners), 0), iota((entries, owners), 1)
    spread = ((entry >= owner * slots) & (entry < (owner + 1) * slots)).astype(F32)
    mine = lax.rem(iota((entries, slots), 0), slots) == iota((entries, slots), 1)

    def column(ref):
        wide = jnp.dot(spread, ref[...].astype(F32), precision=lax.Precision.HIGHEST)
        return jnp.sum(jnp.where(mine, wide, 0.0), axis=1, keepdims=True).astype(jnp.int32)

    local = iota((1, count), 1)
    give = one_hot(column(send_ref), local)
    put_ref[...] = (column(dest_ref) == local).astype(F32).T.astype(BF16)
    want = column(want_ref)
    full_ref[...] = want

    named = (want == iota((1, xlines * count), 1)).astype(F32)
    counts = dot(jnp.ones((8, entries), BF16), named.astype(BF16))
    used = jnp.concatenate([counts[:1, tile_at(b, count)] for b in range(xlines)], axis=0) > 0.5
    used = used.astype(F32)
    earlier = (iota((count, count), 0) < iota((count, count), 1)).astype(F32).astype(BF16)
    rank = dot(used.astype(BF16), earlier)
    most = jnp.max(jnp.max(rank + used, axis=1, keepdims=True), axis=0, keepdims=True)
    over = (most > ROOM).astype(F32)
    places = jnp.concatenate([rank[b : b + 1] + float(b * ROOM) for b in range(xlines)], axis=1)
    place = jnp.sum(named * places, axis=1, keepdims=True).astype(jnp.int32)
    fast_ref[...] = jnp.where(want < 0, -1, place)
    pack = ((iota((ROOM, count), 0).astype(F32) == rank[:1]) & (used[:1] > 0.5)).astype(F32).astype(BF16)

    first.wait()
    odd = lax.rem(iota((1, length), 1), 2) == 1
    own = rec[...].astype(F32)
    both = jnp.concatenate([jnp.where(odd, 0.0, own), jnp.where(odd, own, 0.0)], axis=0).astype(BF16)
    for copy in coming:
        copy.wait()
    lane = iota((1, TILE), 1)
    for j in range(quarter // TILE):
        cos = dot(both, table[:, tile_at(j)])
        sin = dot(both, table[:, quarter + j * TILE : quarter + (j + 1) * TILE])
        cos_even, cos_odd, sin_even, sin_odd = cos[:count], cos[count:], sin[:count], sin[count:]
        parts = [cos_even + cos_odd, cos_even - cos_odd, sin_even + sin_odd, sin_odd - sin_even]
        if j == 0:
            parts[1] = jnp.where(lane == 0, sin_even, parts[1])
            parts[2] = jnp.where(lane == 0, 0.0, parts[2])
            parts[3] = jnp.where(lane == 0, sin_odd, parts[3])
        for p, part in enumerate(parts):
            spec[:, p * quarter + j * TILE : p * quarter + (j + 1) * TILE] = part.astype(BF16)
    going = [start(spec, spec_hbm, sems.at[1])]
    for j in range(length // TILE):
        packed[:, tile_at(j)] = dot(pack, spec[:, tile_at(j)]).astype(BF16)
    base = 0
    for i, size in enumerate(CHUNKS):
        going.append(start(packed.at[base : base + size], packed_hbm[i], packed_sems.at[i]))
        base += size
    for j in range(length // TILE):
        rows = dot(give, spec[:, tile_at(j)])
        if j * TILE == 2 * quarter:
            rows = jnp.where(lane == 0, over, rows)
        out[j] = rows.astype(BF16)
        going.append(start(out.at[j], out_hbm.at[:, tile_at(j)], out_sems.at[j]))
    for copy in going:
        copy.wait()


def open_rows(send, want, dest, records, table, xlines):
    count, length = records.shape
    entries = send.size
    steps = length // TILE
    return pl.pallas_call(
        functools.partial(open_kernel, xlines),
        in_specs=[VMEM] * 3 + [ANY] * 2,
        out_specs=[ANY] * (2 + len(CHUNKS)) + [VMEM] * 3,
        out_shape=[
            jax.ShapeDtypeStruct((entries, length), BF16),
            *[jax.ShapeDtypeStruct((size, length), BF16) for size in CHUNKS],
            jax.ShapeDtypeStruct((count, length), BF16),
            jax.ShapeDtypeStruct((entries, 1), jnp.int32),
            jax.ShapeDtypeStruct((entries, 1), jnp.int32),
            jax.ShapeDtypeStruct((count, entries), BF16),
        ],
        scratch_shapes=[
            pltpu.VMEM((count, length), BF16),
            pltpu.VMEM(table.shape, BF16),
            pltpu.VMEM((count, length), BF16),
            pltpu.VMEM((steps, entries, TILE), BF16),
            pltpu.VMEM((ROOM, length), BF16),
            pltpu.SemaphoreType.DMA((2,)),
            pltpu.SemaphoreType.DMA((steps,)),
            pltpu.SemaphoreType.DMA((len(CHUNKS),)),
            pltpu.SemaphoreType.DMA((2,)),
        ],
        compiler_params=PARAMS,
    )(send, want, dest, records, table)


def close_kernel(want_ref, put_ref, inverse_hbm, received_hbm, *refs):
    *chunks, out_ref, rows, received, inverse, total, rows_sems, sems = refs
    length = inverse.shape[1]
    quarter = length // 4
    coming, base = [], 0
    for i, chunk in enumerate(chunks):
        size = chunk.shape[0]
        coming.append(start(chunk, rows.at[base : base + size], rows_sems.at[i]))
        base += size
    other = start(received_hbm, received, sems.at[0])
    take = one_hot(want_ref[...], iota((1, rows.shape[0]), 1))
    for copy in coming:
        copy.wait()
    pieces = [start(inverse_hbm, inverse, sems.at[1])]
    put = put_ref[...]
    count = put.shape[0]
    lane = iota((1, TILE), 1)
    other.wait()
    stacks = []
    for j in range(quarter // TILE):
        sums = []
        for mirror in range(2):
            at = mirror * quarter + j * TILE
            re, im = slice(at, at + TILE), slice(2 * quarter + at, 2 * quarter + at + TILE)
            a_re, a_im = dot(take, rows[:, re]), dot(take, rows[:, im])
            b_re, b_im = received[:, re].astype(F32), received[:, im].astype(F32)
            for product in (a_re * b_re - a_im * b_im, a_re * b_im + a_im * b_re):
                high = product.astype(BF16)
                low = (product - high.astype(F32)).astype(BF16)
                sums.append((dot(put, high) + dot(put, low)).astype(BF16).astype(F32))
        re, im, mirror_re, mirror_im = sums
        even_re, odd_re, even_im, odd_im = re + mirror_re, re - mirror_re, im - mirror_im, im + mirror_im
        if j == 0:
            even_re, odd_re = jnp.where(lane == 0, re, even_re), jnp.where(lane == 0, re, odd_re)
            even_im, odd_im = jnp.where(lane == 0, mirror_re, even_im), jnp.where(lane == 0, mirror_im, odd_im)
        stacks.append(
            [jnp.concatenate(pair, axis=0).astype(BF16) for pair in ((even_re, odd_re), (even_im, odd_im))]
        )
    for copy in pieces:
        copy.wait()
    odd = lax.rem(iota((1, TILE), 1), 2) == 1
    for c in range(length // TILE):
        acc = None
        for j, pair in enumerate(stacks):
            for p, stack in enumerate(pair):
                at = p * quarter + j * TILE
                part = dot(stack, inverse[at : at + TILE, tile_at(c)])
                acc = part if acc is None else acc + part
        out_ref[:, tile_at(c)] = jnp.where(odd, acc[count:], acc[:count])


def close(want, put, inverse, received, chunks):
    entries, length = received.shape
    return pl.pallas_call(
        close_kernel,
        in_specs=[VMEM] * 2 + [ANY] * (2 + len(chunks)),
        out_specs=VMEM,
        out_shape=jax.ShapeDtypeStruct((put.shape[0], length), F32),
        scratch_shapes=[
            pltpu.VMEM((sum(c.shape[0] for c in chunks), length), BF16),
            pltpu.VMEM((entries, length), BF16),
            pltpu.VMEM(inverse.shape, BF16),
            pltpu.VMEM((8, 128), F32),
            pltpu.SemaphoreType.DMA((len(chunks),)),
            pltpu.SemaphoreType.DMA((2,)),
        ],
        compiler_params=PARAMS,
    )(want, put, inverse, received, *chunks)


def ring(parts, xlines):
    up = [(i, (i + 1) % xlines) for i in range(xlines)]
    down = [(i, (i - 1) % xlines) for i in range(xlines)]
    half = xlines // 2
    below, above = list(parts), list(parts)
    chunks = {(0, s): part for s, part in enumerate(parts)}
    for step in range(1, half + 1):
        for s in range(2):
            if step < half or s == 0:
                below[s] = chunks[xlines - step, s] = lax.ppermute(below[s], "xline", up)
            if step < half or s == 1:
                above[s] = chunks[step, s] = lax.ppermute(above[s], "xline", down)
    return [chunks[o, s] for o in range(xlines) for s in range(2)]


def on_device(forward, inverse, records, source_trace, target_trace, mirror, live_slots):
    shot_dev, rx_local, length = records.shape
    count = shot_dev * rx_local
    xlines = lax.axis_size("xline")
    me, line = lax.axis_index("shot"), lax.axis_index("xline")
    owners, _, slots = source_trace.shape

    send = lax.dynamic_index_in_dim(source_trace, me, 1, False)
    r_local = lax.dynamic_index_in_dim(source_trace, me, 0, False) % rx_local
    targets, mirrors = target_trace[0], mirror[0]
    live = jnp.arange(slots, dtype=jnp.int32)[None, :] < live_slots[0][:, None]
    offset = (mirrors // rx_local - line) % xlines
    want = jnp.where(live, offset * count + targets * rx_local + mirrors % rx_local, -1)
    dest = jnp.where(live, targets * rx_local + r_local, -1)
    outgoing, *packed, spectra, full, fast, put = open_rows(
        send, want, dest, records.reshape(count, length), forward, xlines
    )
    received = lax.all_to_all(
        outgoing.reshape(owners, slots, length), "shot", split_axis=0, concat_axis=0, tiled=True
    ).reshape(owners * slots, length)
    chunks = ring(packed, xlines)
    over = jnp.any(received[::slots, length // 2] != 0)

    def whole(received, spectra, full, fast, put, chunks):
        parts = [spectra[: count // 2], spectra[count // 2 :]]
        return close(full, put, inverse, received, ring(parts, xlines))

    def short(received, spectra, full, fast, put, chunks):
        return close(fast, put, inverse, received, chunks)

    predicted = lax.cond(over, whole, short, received, spectra, full, fast, put, chunks)
    return predicted.reshape(shot_dev, rx_local, length)


def solution(mesh):
    placed = (
        P("shot", "xline", None),
        P(),
        P("shot", None, None),
        P("shot", None, None),
        P("shot", None),
    )

    def run(*args):
        forward, inverse = tables(args[0].shape[-1])
        return jax.shard_map(
            on_device,
            mesh=mesh,
            in_specs=(P(), P(), *placed),
            out_specs=P("shot", "xline", None),
            check_vma=False,
        )(jnp.asarray(forward), jnp.asarray(inverse), *args)

    return run
```

```python
import functools
import math

import jax
import jax.numpy as jnp
import numpy as np
from jax import lax
from jax.experimental import pallas as pl
from jax.experimental.pallas import tpu as pltpu
from jax.sharding import PartitionSpec as P

PARAMS = pltpu.CompilerParams(vmem_limit_bytes=56 * 1024 * 1024)
VMEM = pl.BlockSpec(memory_space=pltpu.VMEM)
ANY = pl.BlockSpec(memory_space=pl.ANY)
TILE = 256
F32 = jnp.float32
BF16 = jnp.bfloat16
CHUNKS = (48, 32)
ROOM = sum(CHUNKS)


def tables(length):
    quarter = length // 4
    t = np.arange(length, dtype=np.int64)[:, None]
    f = np.arange(quarter, dtype=np.int64)[None, :]
    phase = (t * f % length).astype(np.float64) * (2.0 * math.pi / length)
    cos, sin = np.cos(phase), -np.sin(phase)
    turn = t[:, 0] % 4
    sin[:, 0] = np.array([1.0, -1.0, -1.0, 1.0])[turn]
    forward = np.concatenate([cos, sin], axis=1)
    weight = np.full(2 * quarter, 2.0 / length)
    weight[0] = 1.0 / length
    inverse = (forward * weight).T
    return forward.astype(BF16), inverse.astype(BF16)


def dot(left, right):
    return jnp.dot(left, right, preferred_element_type=F32)


def one_hot(left, right):
    return (left == right).astype(F32).astype(BF16)


def iota(shape, axis):
    return lax.broadcasted_iota(jnp.int32, shape, axis)


def tile_at(j, tile=TILE):
    return slice(j * tile, (j + 1) * tile)


def start(source, target, sem):
    copy = pltpu.make_async_copy(source, target, sem)
    copy.start()
    return copy


def open_kernel(xlines, shots, source_ref, target_ref, mirror_ref, live_ref, rec_hbm, table_hbm, *refs):
    out_hbm, *packed_hbm, spec_hbm, full_ref, fast_ref, put_ref = refs[: 5 + len(CHUNKS)]
    rec, table, spec, out, packed, table_sems, out_sems, packed_sems, sems = refs[5 + len(CHUNKS) :]
    count, length = rec.shape
    quarter = length // 4
    first = start(rec_hbm, rec, sems.at[0])
    half = table.shape[0] // 2
    halves = [pl.ds(i * half, half) for i in range(2)]
    coming = [start(table_hbm.at[h], table.at[h], table_sems.at[i]) for i, h in enumerate(halves)]

    me, line = lax.axis_index("shot"), lax.axis_index("xline")
    slots, owners = target_ref.shape
    entries = owners * slots
    spread = (lax.rem(iota((entries, slots), 0), slots) == iota((entries, slots), 1)).astype(F32)
    entry, owner = iota((entries, owners), 0), iota((entries, owners), 1)
    mine = (entry >= owner * slots) & (entry < (owner + 1) * slots)

    def column(values):
        wide = jnp.dot(spread, values.astype(F32), precision=lax.Precision.HIGHEST)
        return jnp.sum(jnp.where(mine, wide, 0.0), axis=1, keepdims=True).astype(jnp.int32)

    local = iota((1, count), 1)
    rx_local = count // shots
    live = iota((slots, owners), 0) < live_ref[...]
    target, mirrored = target_ref[...], mirror_ref[...]
    used_here = source_ref[pl.ds(pl.multiple_of(me * slots, slots), slots), :]
    dest = jnp.where(live, target * rx_local + lax.rem(used_here, rx_local), -1)
    offset = lax.rem(lax.div(mirrored, rx_local) + xlines - line, xlines)
    want = jnp.where(live, offset * count + target * rx_local + lax.rem(mirrored, rx_local), -1)
    send = jnp.sum(jnp.where(owner == me, source_ref[...], 0), axis=1, keepdims=True)
    give = one_hot(send, local)
    put_ref[...] = (column(dest) == local).astype(F32).T.astype(BF16)
    want = column(want)
    full_ref[...] = want

    named = (want == iota((1, xlines * count), 1)).astype(F32)
    counts = dot(jnp.ones((8, entries), BF16), named.astype(BF16))
    used = jnp.concatenate([counts[:1, tile_at(b, count)] for b in range(xlines)], axis=0) > 0.5
    used = used.astype(F32)
    earlier = (iota((count, count), 0) < iota((count, count), 1)).astype(F32).astype(BF16)
    rank = dot(used.astype(BF16), earlier)
    most = jnp.max(jnp.max(rank + used, axis=1, keepdims=True), axis=0, keepdims=True)
    over = (most > ROOM).astype(F32)
    places = jnp.concatenate([rank[b : b + 1] + float(b * ROOM) for b in range(xlines)], axis=1)
    place = jnp.sum(named * places, axis=1, keepdims=True).astype(jnp.int32)
    fast_ref[...] = jnp.where(want < 0, -1, place)
    pack = ((iota((ROOM, count), 0).astype(F32) == rank[:1]) & (used[:1] > 0.5)).astype(F32).astype(BF16)

    first.wait()
    odd = lax.rem(iota((1, length), 1), 2) == 1
    own = rec[...].astype(F32)
    both = jnp.concatenate([jnp.where(odd, 0.0, own), jnp.where(odd, own, 0.0)], axis=0).astype(BF16)
    for copy in coming:
        copy.wait()
    lane = iota((1, TILE), 1)
    for j in range(quarter // TILE):
        cos = dot(both, table[:, tile_at(j)])
        sin = dot(both, table[:, quarter + j * TILE : quarter + (j + 1) * TILE])
        cos_even, cos_odd, sin_even, sin_odd = cos[:count], cos[count:], sin[:count], sin[count:]
        parts = [cos_even + cos_odd, cos_even - cos_odd, sin_even + sin_odd, sin_odd - sin_even]
        if j == 0:
            parts[1] = jnp.where(lane == 0, sin_even, parts[1])
            parts[2] = jnp.where(lane == 0, 0.0, parts[2])
            parts[3] = jnp.where(lane == 0, sin_odd, parts[3])
        for p, part in enumerate(parts):
            spec[:, p * quarter + j * TILE : p * quarter + (j + 1) * TILE] = part.astype(BF16)
    going = [start(spec, spec_hbm, sems.at[1])]
    for j in range(length // TILE):
        packed[:, tile_at(j)] = dot(pack, spec[:, tile_at(j)]).astype(BF16)
    base = 0
    for i, size in enumerate(CHUNKS):
        going.append(start(packed.at[base : base + size], packed_hbm[i], packed_sems.at[i]))
        base += size
    for j in range(length // TILE):
        rows = dot(give, spec[:, tile_at(j)])
        if j * TILE == 2 * quarter:
            rows = jnp.where(lane == 0, over, rows)
        out[j] = rows.astype(BF16)
        going.append(start(out.at[j], out_hbm.at[:, tile_at(j)], out_sems.at[j]))
    for copy in going:
        copy.wait()


def open_rows(source, target, mirror, live, records, table, xlines, shots):
    count, length = records.shape
    entries = source.shape[0]
    steps = length // TILE
    return pl.pallas_call(
        functools.partial(open_kernel, xlines, shots),
        in_specs=[VMEM] * 4 + [ANY] * 2,
        out_specs=[ANY] * (2 + len(CHUNKS)) + [VMEM] * 3,
        out_shape=[
            jax.ShapeDtypeStruct((entries, length), BF16),
            *[jax.ShapeDtypeStruct((size, length), BF16) for size in CHUNKS],
            jax.ShapeDtypeStruct((count, length), BF16),
            jax.ShapeDtypeStruct((entries, 1), jnp.int32),
            jax.ShapeDtypeStruct((entries, 1), jnp.int32),
            jax.ShapeDtypeStruct((count, entries), BF16),
        ],
        scratch_shapes=[
            pltpu.VMEM((count, length), BF16),
            pltpu.VMEM(table.shape, BF16),
            pltpu.VMEM((count, length), BF16),
            pltpu.VMEM((steps, entries, TILE), BF16),
            pltpu.VMEM((ROOM, length), BF16),
            pltpu.SemaphoreType.DMA((2,)),
            pltpu.SemaphoreType.DMA((steps,)),
            pltpu.SemaphoreType.DMA((len(CHUNKS),)),
            pltpu.SemaphoreType.DMA((2,)),
        ],
        compiler_params=PARAMS,
    )(source, target, mirror, live, records, table)


def close_kernel(want_ref, put_ref, inverse_hbm, received_hbm, *refs):
    *chunks, out_ref, rows, received, inverse, rows_sems, sems = refs
    length = inverse.shape[1]
    quarter = length // 4
    coming, base = [], 0
    for i, chunk in enumerate(chunks):
        size = chunk.shape[0]
        coming.append(start(chunk, rows.at[base : base + size], rows_sems.at[i]))
        base += size
    other = start(received_hbm, received, sems.at[0])
    take = one_hot(want_ref[...], iota((1, rows.shape[0]), 1))
    for copy in coming:
        copy.wait()
    pieces = [start(inverse_hbm, inverse, sems.at[1])]
    put = put_ref[...]
    count = put.shape[0]
    lane = iota((1, TILE), 1)
    other.wait()
    stacks = []
    for j in range(quarter // TILE):
        sums = []
        for mirror in range(2):
            at = mirror * quarter + j * TILE
            re, im = slice(at, at + TILE), slice(2 * quarter + at, 2 * quarter + at + TILE)
            a_re, a_im = dot(take, rows[:, re]), dot(take, rows[:, im])
            b_re, b_im = received[:, re].astype(F32), received[:, im].astype(F32)
            for product in (a_re * b_re - a_im * b_im, a_re * b_im + a_im * b_re):
                high = product.astype(BF16)
                low = (product - high.astype(F32)).astype(BF16)
                sums.append((dot(put, high) + dot(put, low)).astype(BF16).astype(F32))
        re, im, mirror_re, mirror_im = sums
        even_re, odd_re, even_im, odd_im = re + mirror_re, re - mirror_re, im - mirror_im, im + mirror_im
        if j == 0:
            even_re, odd_re = jnp.where(lane == 0, re, even_re), jnp.where(lane == 0, re, odd_re)
            even_im, odd_im = jnp.where(lane == 0, mirror_re, even_im), jnp.where(lane == 0, mirror_im, odd_im)
        stacks.append(
            [jnp.concatenate(pair, axis=0).astype(BF16) for pair in ((even_re, odd_re), (even_im, odd_im))]
        )
    pieces[0].wait()
    odd = lax.rem(iota((1, TILE), 1), 2) == 1
    for c in range(length // TILE):
        acc = None
        for j, pair in enumerate(stacks):
            for p, stack in enumerate(pair):
                at = p * quarter + j * TILE
                part = dot(stack, inverse[at : at + TILE, tile_at(c)])
                acc = part if acc is None else acc + part
        out_ref[:, tile_at(c)] = jnp.where(odd, acc[count:], acc[:count])


def close(want, put, inverse, received, chunks):
    entries, length = received.shape
    return pl.pallas_call(
        close_kernel,
        in_specs=[VMEM] * 2 + [ANY] * (2 + len(chunks)),
        out_specs=VMEM,
        out_shape=jax.ShapeDtypeStruct((put.shape[0], length), F32),
        scratch_shapes=[
            pltpu.VMEM((sum(c.shape[0] for c in chunks), length), BF16),
            pltpu.VMEM((entries, length), BF16),
            pltpu.VMEM(inverse.shape, BF16),
            pltpu.SemaphoreType.DMA((len(chunks),)),
            pltpu.SemaphoreType.DMA((2,)),
        ],
        compiler_params=PARAMS,
    )(want, put, inverse, received, *chunks)


def ring(parts, xlines):
    up = [(i, (i + 1) % xlines) for i in range(xlines)]
    down = [(i, (i - 1) % xlines) for i in range(xlines)]
    half = xlines // 2
    below, above = list(parts), list(parts)
    chunks = {(0, s): part for s, part in enumerate(parts)}
    for step in range(1, half + 1):
        for s in range(2):
            if step < half or s == 0:
                below[s] = chunks[xlines - step, s] = lax.ppermute(below[s], "xline", up)
            if step < half or s == 1:
                above[s] = chunks[step, s] = lax.ppermute(above[s], "xline", down)
    return [chunks[o, s] for o in range(xlines) for s in range(2)]


def on_device(forward, inverse, records, source_trace, target_trace, mirror, live_slots):
    shot_dev, rx_local, length = records.shape
    count = shot_dev * rx_local
    xlines = lax.axis_size("xline")
    owners, _, slots = source_trace.shape
    source = source_trace.transpose(0, 2, 1).reshape(owners * slots, owners)
    outgoing, *packed, spectra, full, fast, put = open_rows(
        source,
        target_trace[0].T,
        mirror[0].T,
        live_slots,
        records.reshape(count, length),
        forward,
        xlines,
        shot_dev,
    )
    received = lax.all_to_all(
        outgoing.reshape(owners, slots, length), "shot", split_axis=0, concat_axis=0, tiled=True
    ).reshape(owners * slots, length)
    chunks = ring(packed, xlines)
    over = jnp.any(received[::slots, length // 2] != 0)

    def whole(received, spectra, full, fast, put, chunks):
        parts = [spectra[: count // 2], spectra[count // 2 :]]
        return close(full, put, inverse, received, ring(parts, xlines))

    def short(received, spectra, full, fast, put, chunks):
        return close(fast, put, inverse, received, chunks)

    predicted = lax.cond(over, whole, short, received, spectra, full, fast, put, chunks)
    return predicted.reshape(shot_dev, rx_local, length)


def solution(mesh):
    placed = (
        P("shot", "xline", None),
        P(),
        P("shot", None, None),
        P("shot", None, None),
        P("shot", None),
    )

    def run(*args):
        forward, inverse = tables(args[0].shape[-1])
        return jax.shard_map(
            on_device,
            mesh=mesh,
            in_specs=(P(), P(), *placed),
            out_specs=P("shot", "xline", None),
            check_vma=False,
        )(jnp.asarray(forward), jnp.asarray(inverse), *args)

    return run
```

```python
import functools
import math

import jax
import jax.numpy as jnp
import numpy as np
from jax import lax
from jax.experimental import pallas as pl
from jax.experimental.pallas import tpu as pltpu
from jax.sharding import PartitionSpec as P

PARAMS = pltpu.CompilerParams(vmem_limit_bytes=56 * 1024 * 1024)
VMEM = pl.BlockSpec(memory_space=pltpu.VMEM)
ANY = pl.BlockSpec(memory_space=pl.ANY)
TILE = 256
F32 = jnp.float32
BF16 = jnp.bfloat16
ROOM = 80
PARTS = 2


def tables(length):
    quarter = length // 4
    t = np.arange(length, dtype=np.int64)[:, None]
    f = np.arange(quarter, dtype=np.int64)[None, :]
    phase = (t * f % length).astype(np.float64) * (2.0 * math.pi / length)
    cos, sin = np.cos(phase), -np.sin(phase)
    turn = t[:, 0] % 4
    sin[:, 0] = np.array([1.0, -1.0, -1.0, 1.0])[turn]
    forward = np.concatenate([cos, sin], axis=1)
    weight = np.full(2 * quarter, 2.0 / length)
    weight[0] = 1.0 / length
    inverse = (forward * weight).T
    return forward.astype(BF16), inverse.astype(BF16)


def dot(left, right):
    return jnp.dot(left, right, preferred_element_type=F32)


def one_hot(left, right):
    return (left == right).astype(F32).astype(BF16)


def iota(shape, axis):
    return lax.broadcasted_iota(jnp.int32, shape, axis)


def tile_at(j, tile=TILE):
    return slice(j * tile, (j + 1) * tile)


def start(source, target, sem):
    copy = pltpu.make_async_copy(source, target, sem)
    copy.start()
    return copy


def open_kernel(xlines, shots, source_hbm, target_hbm, mirror_hbm, live_hbm, rec_hbm, table_hbm, *refs):
    out_hbm, *parts_hbm = refs[: 1 + 2 * PARTS]
    lists_hbm = refs[1 + 2 * PARTS : 4 + 2 * PARTS]
    source_ref, target_ref, mirror_ref, live_ref, rec, table, spec, out, packed, *lists = refs[4 + 2 * PARTS : -4]
    index_sems, table_sems, out_sems, sems = refs[-4:]
    count, length = rec.shape
    quarter = length // 4
    indices = [
        start(source, target, index_sems.at[i])
        for i, (source, target) in enumerate(
            (
                (source_hbm, source_ref),
                (target_hbm, target_ref),
                (mirror_hbm, mirror_ref),
                (live_hbm, live_ref),
            )
        )
    ]
    first = start(rec_hbm, rec, sems.at[0])
    half = table.shape[0] // 2
    halves = [pl.ds(i * half, half) for i in range(2)]
    coming = [start(table_hbm.at[h], table.at[h], table_sems.at[i]) for i, h in enumerate(halves)]
    full_ref, fast_ref, put_ref = lists
    for copy in indices:
        copy.wait()

    me, line = lax.axis_index("shot"), lax.axis_index("xline")
    slots, owners = target_ref.shape
    entries = owners * slots
    spread = (lax.rem(iota((entries, slots), 0), slots) == iota((entries, slots), 1)).astype(F32)
    entry, owner = iota((entries, owners), 0), iota((entries, owners), 1)
    mine = (entry >= owner * slots) & (entry < (owner + 1) * slots)

    def column(values):
        wide = jnp.dot(spread, values.astype(F32), precision=lax.Precision.HIGHEST)
        return jnp.sum(jnp.where(mine, wide, 0.0), axis=1, keepdims=True).astype(jnp.int32)

    local = iota((1, count), 1)
    rx_local = count // shots
    live = iota((slots, owners), 0) < live_ref[...]
    target, mirrored = target_ref[...], mirror_ref[...]
    used_here = source_ref[pl.ds(pl.multiple_of(me * slots, slots), slots), :]
    dest = jnp.where(live, target * rx_local + lax.rem(used_here, rx_local), -1)
    offset = lax.rem(lax.div(mirrored, rx_local) + xlines - line, xlines)
    want = jnp.where(live, offset * count + target * rx_local + lax.rem(mirrored, rx_local), -1)
    send = jnp.sum(jnp.where(owner == me, source_ref[...], 0), axis=1, keepdims=True)
    give = one_hot(send, local)
    put_ref[...] = (column(dest) == local).astype(F32).T.astype(BF16)
    want = column(want)
    full_ref[...] = want

    named = (want == iota((1, xlines * count), 1)).astype(F32)
    counts = dot(jnp.ones((8, entries), BF16), named.astype(BF16))
    used = jnp.concatenate([counts[:1, tile_at(b, count)] for b in range(xlines)], axis=0) > 0.5
    used = used.astype(F32)
    earlier = (iota((count, count), 0) < iota((count, count), 1)).astype(F32).astype(BF16)
    rank = dot(used.astype(BF16), earlier)
    most = jnp.max(jnp.max(rank + used, axis=1, keepdims=True), axis=0, keepdims=True)
    over = (most > ROOM).astype(F32)
    places = jnp.concatenate([rank[b : b + 1] + float(b * ROOM) for b in range(xlines)], axis=1)
    place = jnp.sum(named * places, axis=1, keepdims=True).astype(jnp.int32)
    fast_ref[...] = jnp.where(want < 0, -1, place)
    pack = ((iota((ROOM, count), 0).astype(F32) == rank[:1]) & (used[:1] > 0.5)).astype(F32).astype(BF16)

    first.wait()
    odd = lax.rem(iota((1, length), 1), 2) == 1
    own = rec[...].astype(F32)
    both = jnp.concatenate([jnp.where(odd, 0.0, own), jnp.where(odd, own, 0.0)], axis=0).astype(BF16)
    for copy in coming:
        copy.wait()
    lane = iota((1, TILE), 1)
    for j in range(quarter // TILE):
        cos = dot(both, table[:, tile_at(j)])
        sin = dot(both, table[:, quarter + j * TILE : quarter + (j + 1) * TILE])
        cos_even, cos_odd, sin_even, sin_odd = cos[:count], cos[count:], sin[:count], sin[count:]
        parts = [cos_even + cos_odd, cos_even - cos_odd, sin_even + sin_odd, sin_odd - sin_even]
        if j == 0:
            parts[1] = jnp.where(lane == 0, sin_even, parts[1])
            parts[2] = jnp.where(lane == 0, 0.0, parts[2])
            parts[3] = jnp.where(lane == 0, sin_odd, parts[3])
        for p, part in enumerate(parts):
            spec[:, p * quarter + j * TILE : p * quarter + (j + 1) * TILE] = part.astype(BF16)
    for j in range(length // TILE):
        packed[:, tile_at(j)] = dot(pack, spec[:, tile_at(j)]).astype(BF16)
    going = [start(ref, hbm, index_sems.at[i]) for i, (ref, hbm) in enumerate(zip(lists, lists_hbm))]
    for p in range(PARTS):
        columns = tile_at(p, length // PARTS)
        going.append(start(packed.at[:, columns], parts_hbm[p], sems.at[1 + p]))
        going.append(start(spec.at[:, columns], parts_hbm[PARTS + p], sems.at[1 + PARTS + p]))
    for j in range(length // TILE):
        rows = dot(give, spec[:, tile_at(j)])
        if j * TILE == 2 * quarter:
            rows = jnp.where(lane == 0, over, rows)
        out[j] = rows.astype(BF16)
        going.append(start(out.at[j], out_hbm.at[:, tile_at(j)], out_sems.at[j]))
    for copy in going:
        copy.wait()


def open_rows(source, target, mirror, live, records, table, xlines, shots):
    count, length = records.shape
    entries = source.shape[0]
    steps = length // TILE
    lists = [
        jax.ShapeDtypeStruct((entries, 1), jnp.int32),
        jax.ShapeDtypeStruct((entries, 1), jnp.int32),
        jax.ShapeDtypeStruct((count, entries), BF16),
    ]
    return pl.pallas_call(
        functools.partial(open_kernel, xlines, shots),
        in_specs=[ANY] * 6,
        out_specs=[ANY] * (1 + 2 * PARTS + len(lists)),
        out_shape=[
            jax.ShapeDtypeStruct((entries, length), BF16),
            *[jax.ShapeDtypeStruct((ROOM, length // PARTS), BF16)] * PARTS,
            *[jax.ShapeDtypeStruct((count, length // PARTS), BF16)] * PARTS,
            *lists,
        ],
        scratch_shapes=[
            pltpu.VMEM(source.shape, jnp.int32),
            pltpu.VMEM(target.shape, jnp.int32),
            pltpu.VMEM(mirror.shape, jnp.int32),
            pltpu.VMEM(live.shape, jnp.int32),
            pltpu.VMEM((count, length), BF16),
            pltpu.VMEM(table.shape, BF16),
            pltpu.VMEM((count, length), BF16),
            pltpu.VMEM((steps, entries, TILE), BF16),
            pltpu.VMEM((ROOM, length), BF16),
            *[pltpu.VMEM(l.shape, l.dtype) for l in lists],
            pltpu.SemaphoreType.DMA((4,)),
            pltpu.SemaphoreType.DMA((2,)),
            pltpu.SemaphoreType.DMA((steps,)),
            pltpu.SemaphoreType.DMA((1 + 2 * PARTS,)),
        ],
        compiler_params=PARAMS,
    )(source, target, mirror, live, records, table)


def close_kernel(want_hbm, put_hbm, inverse_hbm, received_hbm, *refs):
    *chunks, out_ref, want_ref, put_ref, rows, received, inverse, rows_sems, sems = refs
    length = inverse.shape[1]
    quarter = length // 4
    size, columns = chunks[0].shape
    lists = [start(want_hbm, want_ref, sems.at[0]), start(put_hbm, put_ref, sems.at[1])]
    coming = []
    for i, chunk in enumerate(chunks):
        block, part = i // PARTS, i % PARTS
        place = rows.at[block * size : (block + 1) * size, part * columns : (part + 1) * columns]
        coming.append(start(chunk, place, rows_sems.at[i]))
    other = start(received_hbm, received, sems.at[2])
    table = start(inverse_hbm, inverse, sems.at[3])
    for copy in lists:
        copy.wait()
    take = one_hot(want_ref[...], iota((1, rows.shape[0]), 1))
    for copy in coming:
        copy.wait()
    put = put_ref[...]
    count = put.shape[0]
    lane = iota((1, TILE), 1)
    other.wait()
    stacks = []
    for j in range(quarter // TILE):
        sums = []
        for mirror in range(2):
            at = mirror * quarter + j * TILE
            re, im = slice(at, at + TILE), slice(2 * quarter + at, 2 * quarter + at + TILE)
            a_re, a_im = dot(take, rows[:, re]), dot(take, rows[:, im])
            b_re, b_im = received[:, re].astype(F32), received[:, im].astype(F32)
            for product in (a_re * b_re - a_im * b_im, a_re * b_im + a_im * b_re):
                high = product.astype(BF16)
                sums.append(dot(put, high).astype(BF16).astype(F32))
        re, im, mirror_re, mirror_im = sums
        even_re, odd_re, even_im, odd_im = re + mirror_re, re - mirror_re, im - mirror_im, im + mirror_im
        if j == 0:
            even_re, odd_re = jnp.where(lane == 0, re, even_re), jnp.where(lane == 0, re, odd_re)
            even_im, odd_im = jnp.where(lane == 0, mirror_re, even_im), jnp.where(lane == 0, mirror_im, odd_im)
        stacks.append(
            [jnp.concatenate(pair, axis=0).astype(BF16) for pair in ((even_re, odd_re), (even_im, odd_im))]
        )
    table.wait()
    odd = lax.rem(iota((1, TILE), 1), 2) == 1
    for c in range(length // TILE):
        acc = None
        for j, pair in enumerate(stacks):
            for p, stack in enumerate(pair):
                at = p * quarter + j * TILE
                part = dot(stack, inverse[at : at + TILE, tile_at(c)])
                acc = part if acc is None else acc + part
        out_ref[:, tile_at(c)] = jnp.where(odd, acc[count:], acc[:count])


def close(want, put, inverse, received, chunks):
    entries, length = received.shape
    return pl.pallas_call(
        close_kernel,
        in_specs=[ANY] * (4 + len(chunks)),
        out_specs=VMEM,
        out_shape=jax.ShapeDtypeStruct((put.shape[0], length), F32),
        scratch_shapes=[
            pltpu.VMEM(want.shape, jnp.int32),
            pltpu.VMEM(put.shape, BF16),
            pltpu.VMEM((len(chunks) // PARTS * chunks[0].shape[0], length), BF16),
            pltpu.VMEM((entries, length), BF16),
            pltpu.VMEM(inverse.shape, BF16),
            pltpu.SemaphoreType.DMA((len(chunks),)),
            pltpu.SemaphoreType.DMA((4,)),
        ],
        compiler_params=PARAMS,
    )(want, put, inverse, received, *chunks)


def ring(parts, xlines):
    up = [(i, (i + 1) % xlines) for i in range(xlines)]
    down = [(i, (i - 1) % xlines) for i in range(xlines)]
    half = xlines // 2
    below, above = list(parts), list(parts)
    chunks = {(0, s): part for s, part in enumerate(parts)}
    for step in range(1, half + 1):
        for s in range(2):
            if step < half or s == 0:
                below[s] = chunks[xlines - step, s] = lax.ppermute(below[s], "xline", up)
            if step < half or s == 1:
                above[s] = chunks[step, s] = lax.ppermute(above[s], "xline", down)
    return [chunks[o, s] for o in range(xlines) for s in range(2)]


def on_device(forward, inverse, records, source_trace, target_trace, mirror, live_slots):
    shot_dev, rx_local, length = records.shape
    count = shot_dev * rx_local
    xlines = lax.axis_size("xline")
    owners, _, slots = source_trace.shape
    source = source_trace.transpose(0, 2, 1).reshape(owners * slots, owners)
    outgoing, *parts, full, fast, put = open_rows(
        source,
        target_trace[0].T,
        mirror[0].T,
        live_slots,
        records.reshape(count, length),
        forward,
        xlines,
        shot_dev,
    )
    received = lax.all_to_all(
        outgoing.reshape(owners, slots, length), "shot", split_axis=0, concat_axis=0, tiled=True
    ).reshape(owners * slots, length)
    chunks = ring(parts[:PARTS], xlines)
    over = jnp.any(received[::slots, length // 2] != 0)

    def whole(received, spectra, full, fast, put, chunks):
        return close(full, put, inverse, received, ring(spectra, xlines))

    def short(received, spectra, full, fast, put, chunks):
        return close(fast, put, inverse, received, chunks)

    predicted = lax.cond(over, whole, short, received, parts[PARTS:], full, fast, put, chunks)
    return predicted.reshape(shot_dev, rx_local, length)


def solution(mesh):
    placed = (
        P("shot", "xline", None),
        P(),
        P("shot", None, None),
        P("shot", None, None),
        P("shot", None),
    )

    def run(*args):
        forward, inverse = tables(args[0].shape[-1])
        return jax.shard_map(
            on_device,
            mesh=mesh,
            in_specs=(P(), P(), *placed),
            out_specs=P("shot", "xline", None),
            check_vma=False,
        )(jnp.asarray(forward), jnp.asarray(inverse), *args)

    return run
```

```python
import functools
import math

import jax
import jax.numpy as jnp
import numpy as np
from jax import lax
from jax.experimental import pallas as pl
from jax.experimental.pallas import tpu as pltpu
from jax.sharding import PartitionSpec as P

PARAMS = pltpu.CompilerParams(vmem_limit_bytes=56 * 1024 * 1024)
VMEM = pl.BlockSpec(memory_space=pltpu.VMEM)
ANY = pl.BlockSpec(memory_space=pl.ANY)
TILE = 256
F32 = jnp.float32
BF16 = jnp.bfloat16
ROOM = 64
PARTS = 2


def tables(length):
    quarter = length // 4
    t = np.arange(length, dtype=np.int64)[:, None]
    f = np.arange(quarter, dtype=np.int64)[None, :]
    phase = (t * f % length).astype(np.float64) * (2.0 * math.pi / length)
    cos, sin = np.cos(phase), -np.sin(phase)
    turn = t[:, 0] % 4
    sin[:, 0] = np.array([1.0, -1.0, -1.0, 1.0])[turn]
    forward = np.concatenate([cos, sin], axis=1)
    weight = np.full(2 * quarter, 2.0 / length)
    weight[0] = 1.0 / length
    inverse = (forward * weight).T
    return forward.astype(BF16), inverse.astype(BF16)


def dot(left, right):
    return jnp.dot(left, right, preferred_element_type=F32)


def one_hot(left, right):
    return (left == right).astype(F32).astype(BF16)


def iota(shape, axis):
    return lax.broadcasted_iota(jnp.int32, shape, axis)


def tile_at(j, tile=TILE):
    return slice(j * tile, (j + 1) * tile)


def start(source, target, sem):
    copy = pltpu.make_async_copy(source, target, sem)
    copy.start()
    return copy


def open_kernel(xlines, shots, source_hbm, target_hbm, mirror_hbm, live_hbm, rec_hbm, table_hbm, *refs):
    out_hbm, *parts_hbm = refs[: 1 + 2 * PARTS]
    lists_hbm = refs[1 + 2 * PARTS : 4 + 2 * PARTS]
    source_ref, target_ref, mirror_ref, live_ref, rec, table, spec, out, packed, *lists = refs[4 + 2 * PARTS : -4]
    index_sems, table_sems, out_sems, sems = refs[-4:]
    count, length = rec.shape
    quarter = length // 4
    indices = [
        start(source, target, index_sems.at[i])
        for i, (source, target) in enumerate(
            (
                (source_hbm, source_ref),
                (target_hbm, target_ref),
                (mirror_hbm, mirror_ref),
                (live_hbm, live_ref),
            )
        )
    ]
    first = start(rec_hbm, rec, sems.at[0])
    half = table.shape[0] // 2
    halves = [pl.ds(i * half, half) for i in range(2)]
    coming = [start(table_hbm.at[h], table.at[h], table_sems.at[i]) for i, h in enumerate(halves)]
    full_ref, fast_ref, put_ref = lists
    for copy in indices:
        copy.wait()

    me, line = lax.axis_index("shot"), lax.axis_index("xline")
    slots, owners = target_ref.shape
    entries = owners * slots
    spread = (lax.rem(iota((entries, slots), 0), slots) == iota((entries, slots), 1)).astype(F32)
    entry, owner = iota((entries, owners), 0), iota((entries, owners), 1)
    mine = (entry >= owner * slots) & (entry < (owner + 1) * slots)

    def column(values):
        wide = jnp.dot(spread, values.astype(F32), precision=lax.Precision.HIGHEST)
        return jnp.sum(jnp.where(mine, wide, 0.0), axis=1, keepdims=True).astype(jnp.int32)

    local = iota((1, count), 1)
    rx_local = count // shots
    live = iota((slots, owners), 0) < live_ref[...]
    target, mirrored = target_ref[...], mirror_ref[...]
    used_here = source_ref[pl.ds(pl.multiple_of(me * slots, slots), slots), :]
    dest = jnp.where(live, target * rx_local + lax.rem(used_here, rx_local), -1)
    offset = lax.rem(lax.div(mirrored, rx_local) + xlines - line, xlines)
    want = jnp.where(live, offset * count + target * rx_local + lax.rem(mirrored, rx_local), -1)
    send = jnp.sum(jnp.where(owner == me, source_ref[...], 0), axis=1, keepdims=True)
    give = one_hot(send, local)
    put_ref[...] = (column(dest) == local).astype(F32).T.astype(BF16)
    want = column(want)
    full_ref[...] = want

    named = (want == iota((1, xlines * count), 1)).astype(F32)
    counts = dot(jnp.ones((8, entries), BF16), named.astype(BF16))
    used = jnp.concatenate([counts[:1, tile_at(b, count)] for b in range(xlines)], axis=0) > 0.5
    used = used.astype(F32)
    earlier = (iota((count, count), 0) < iota((count, count), 1)).astype(F32).astype(BF16)
    rank = dot(used.astype(BF16), earlier)
    most = jnp.max(jnp.max(rank + used, axis=1, keepdims=True), axis=0, keepdims=True)
    over = (most > ROOM).astype(F32)
    places = jnp.concatenate([rank[b : b + 1] + float(b * ROOM) for b in range(xlines)], axis=1)
    place = jnp.sum(named * places, axis=1, keepdims=True).astype(jnp.int32)
    fast_ref[...] = jnp.where(want < 0, -1, place)
    pack = ((iota((ROOM, count), 0).astype(F32) == rank[:1]) & (used[:1] > 0.5)).astype(F32).astype(BF16)

    first.wait()
    odd = lax.rem(iota((1, length), 1), 2) == 1
    own = rec[...].astype(F32)
    both = jnp.concatenate([jnp.where(odd, 0.0, own), jnp.where(odd, own, 0.0)], axis=0).astype(BF16)
    for copy in coming:
        copy.wait()
    lane = iota((1, TILE), 1)
    for j in range(quarter // TILE):
        cos = dot(both, table[:, tile_at(j)])
        sin = dot(both, table[:, quarter + j * TILE : quarter + (j + 1) * TILE])
        cos_even, cos_odd, sin_even, sin_odd = cos[:count], cos[count:], sin[:count], sin[count:]
        parts = [cos_even + cos_odd, cos_even - cos_odd, sin_even + sin_odd, sin_odd - sin_even]
        if j == 0:
            parts[1] = jnp.where(lane == 0, sin_even, parts[1])
            parts[2] = jnp.where(lane == 0, 0.0, parts[2])
            parts[3] = jnp.where(lane == 0, sin_odd, parts[3])
        for p, part in enumerate(parts):
            spec[:, p * quarter + j * TILE : p * quarter + (j + 1) * TILE] = part.astype(BF16)
    for j in range(length // TILE):
        packed[:, tile_at(j)] = dot(pack, spec[:, tile_at(j)]).astype(BF16)
    going = [start(ref, hbm, index_sems.at[i]) for i, (ref, hbm) in enumerate(zip(lists, lists_hbm))]
    for p in range(PARTS):
        columns = tile_at(p, length // PARTS)
        going.append(start(packed.at[:, columns], parts_hbm[p], sems.at[1 + p]))
        going.append(start(spec.at[:, columns], parts_hbm[PARTS + p], sems.at[1 + PARTS + p]))
    for j in range(length // TILE):
        rows = dot(give, spec[:, tile_at(j)])
        if j * TILE == 2 * quarter:
            rows = jnp.where(lane == 0, over, rows)
        out[j] = rows.astype(BF16)
        going.append(start(out.at[j], out_hbm.at[:, tile_at(j)], out_sems.at[j]))
    for copy in going:
        copy.wait()


def open_rows(source, target, mirror, live, records, table, xlines, shots):
    count, length = records.shape
    entries = source.shape[0]
    steps = length // TILE
    lists = [
        jax.ShapeDtypeStruct((entries, 1), jnp.int32),
        jax.ShapeDtypeStruct((entries, 1), jnp.int32),
        jax.ShapeDtypeStruct((count, entries), BF16),
    ]
    return pl.pallas_call(
        functools.partial(open_kernel, xlines, shots),
        in_specs=[ANY] * 6,
        out_specs=[ANY] * (1 + 2 * PARTS + len(lists)),
        out_shape=[
            jax.ShapeDtypeStruct((entries, length), BF16),
            *[jax.ShapeDtypeStruct((ROOM, length // PARTS), BF16)] * PARTS,
            *[jax.ShapeDtypeStruct((count, length // PARTS), BF16)] * PARTS,
            *lists,
        ],
        scratch_shapes=[
            pltpu.VMEM(source.shape, jnp.int32),
            pltpu.VMEM(target.shape, jnp.int32),
            pltpu.VMEM(mirror.shape, jnp.int32),
            pltpu.VMEM(live.shape, jnp.int32),
            pltpu.VMEM((count, length), BF16),
            pltpu.VMEM(table.shape, BF16),
            pltpu.VMEM((count, length), BF16),
            pltpu.VMEM((steps, entries, TILE), BF16),
            pltpu.VMEM((ROOM, length), BF16),
            *[pltpu.VMEM(l.shape, l.dtype) for l in lists],
            pltpu.SemaphoreType.DMA((4,)),
            pltpu.SemaphoreType.DMA((2,)),
            pltpu.SemaphoreType.DMA((steps,)),
            pltpu.SemaphoreType.DMA((1 + 2 * PARTS,)),
        ],
        compiler_params=PARAMS,
    )(source, target, mirror, live, records, table)


def close_kernel(want_hbm, put_hbm, inverse_hbm, received_hbm, *refs):
    *chunks, out_ref, want_ref, put_ref, rows, received, inverse, rows_sems, sems = refs
    length = inverse.shape[1]
    quarter = length // 4
    size, columns = chunks[0].shape
    lists = [start(want_hbm, want_ref, sems.at[0]), start(put_hbm, put_ref, sems.at[1])]
    coming = []
    for i, chunk in enumerate(chunks):
        block, part = i // PARTS, i % PARTS
        place = rows.at[block * size : (block + 1) * size, part * columns : (part + 1) * columns]
        coming.append(start(chunk, place, rows_sems.at[i]))
    other = start(received_hbm, received, sems.at[2])
    table = start(inverse_hbm, inverse, sems.at[3])
    for copy in lists:
        copy.wait()
    take = one_hot(want_ref[...], iota((1, rows.shape[0]), 1))
    for copy in coming:
        copy.wait()
    put = put_ref[...]
    count = put.shape[0]
    lane = iota((1, TILE), 1)
    other.wait()
    stacks = []
    for j in range(quarter // TILE):
        sums = []
        for mirror in range(2):
            at = mirror * quarter + j * TILE
            re, im = slice(at, at + TILE), slice(2 * quarter + at, 2 * quarter + at + TILE)
            a_re, a_im = dot(take, rows[:, re]), dot(take, rows[:, im])
            b_re, b_im = received[:, re].astype(F32), received[:, im].astype(F32)
            for product in (a_re * b_re - a_im * b_im, a_re * b_im + a_im * b_re):
                high = product.astype(BF16)
                sums.append(dot(put, high).astype(BF16).astype(F32))
        re, im, mirror_re, mirror_im = sums
        even_re, odd_re, even_im, odd_im = re + mirror_re, re - mirror_re, im - mirror_im, im + mirror_im
        if j == 0:
            even_re, odd_re = jnp.where(lane == 0, re, even_re), jnp.where(lane == 0, re, odd_re)
            even_im, odd_im = jnp.where(lane == 0, mirror_re, even_im), jnp.where(lane == 0, mirror_im, odd_im)
        stacks.append(
            [jnp.concatenate(pair, axis=0).astype(BF16) for pair in ((even_re, odd_re), (even_im, odd_im))]
        )
    table.wait()
    odd = lax.rem(iota((1, TILE), 1), 2) == 1
    for c in range(length // TILE):
        acc = None
        for j, pair in enumerate(stacks):
            for p, stack in enumerate(pair):
                at = p * quarter + j * TILE
                part = dot(stack, inverse[at : at + TILE, tile_at(c)])
                acc = part if acc is None else acc + part
        out_ref[:, tile_at(c)] = jnp.where(odd, acc[count:], acc[:count])


def close(want, put, inverse, received, chunks):
    entries, length = received.shape
    return pl.pallas_call(
        close_kernel,
        in_specs=[ANY] * (4 + len(chunks)),
        out_specs=VMEM,
        out_shape=jax.ShapeDtypeStruct((put.shape[0], length), F32),
        scratch_shapes=[
            pltpu.VMEM(want.shape, jnp.int32),
            pltpu.VMEM(put.shape, BF16),
            pltpu.VMEM((len(chunks) // PARTS * chunks[0].shape[0], length), BF16),
            pltpu.VMEM((entries, length), BF16),
            pltpu.VMEM(inverse.shape, BF16),
            pltpu.SemaphoreType.DMA((len(chunks),)),
            pltpu.SemaphoreType.DMA((4,)),
        ],
        compiler_params=PARAMS,
    )(want, put, inverse, received, *chunks)


def ring(parts, xlines):
    up = [(i, (i + 1) % xlines) for i in range(xlines)]
    down = [(i, (i - 1) % xlines) for i in range(xlines)]
    half = xlines // 2
    below, above = list(parts), list(parts)
    chunks = {(0, s): part for s, part in enumerate(parts)}
    for step in range(1, half + 1):
        for s in range(2):
            if step < half or s == 0:
                below[s] = chunks[xlines - step, s] = lax.ppermute(below[s], "xline", up)
            if step < half or s == 1:
                above[s] = chunks[step, s] = lax.ppermute(above[s], "xline", down)
    return [chunks[o, s] for o in range(xlines) for s in range(2)]


def on_device(forward, inverse, records, source_trace, target_trace, mirror, live_slots):
    shot_dev, rx_local, length = records.shape
    count = shot_dev * rx_local
    xlines = lax.axis_size("xline")
    owners, _, slots = source_trace.shape
    source = source_trace.transpose(0, 2, 1).reshape(owners * slots, owners)
    outgoing, *parts, full, fast, put = open_rows(
        source,
        target_trace[0].T,
        mirror[0].T,
        live_slots,
        records.reshape(count, length),
        forward,
        xlines,
        shot_dev,
    )
    received = lax.all_to_all(
        outgoing.reshape(owners, slots, length), "shot", split_axis=0, concat_axis=0, tiled=True
    ).reshape(owners * slots, length)
    chunks = ring(parts[:PARTS], xlines)
    over = jnp.any(received[::slots, length // 2] != 0)

    def whole(received, spectra, full, fast, put, chunks):
        return close(full, put, inverse, received, ring(spectra, xlines))

    def short(received, spectra, full, fast, put, chunks):
        return close(fast, put, inverse, received, chunks)

    predicted = lax.cond(over, whole, short, received, parts[PARTS:], full, fast, put, chunks)
    return predicted.reshape(shot_dev, rx_local, length)


def solution(mesh):
    placed = (
        P("shot", "xline", None),
        P(),
        P("shot", None, None),
        P("shot", None, None),
        P("shot", None),
    )

    def run(*args):
        forward, inverse = tables(args[0].shape[-1])
        return jax.shard_map(
            on_device,
            mesh=mesh,
            in_specs=(P(), P(), *placed),
            out_specs=P("shot", "xline", None),
            check_vma=False,
        )(jnp.asarray(forward), jnp.asarray(inverse), *args)

    return run
```

```python
import functools
import math

import jax
import jax.numpy as jnp
import numpy as np
from jax import lax
from jax.experimental import pallas as pl
from jax.experimental.pallas import tpu as pltpu
from jax.sharding import PartitionSpec as P

PARAMS = pltpu.CompilerParams(vmem_limit_bytes=56 * 1024 * 1024)
VMEM = pl.BlockSpec(memory_space=pltpu.VMEM)
ANY = pl.BlockSpec(memory_space=pl.ANY)
TILE = 256
F32 = jnp.float32
BF16 = jnp.bfloat16
ROOM = 64
PARTS = 2


def tables(length):
    quarter = length // 4
    t = np.arange(length, dtype=np.int64)[:, None]
    f = np.arange(quarter, dtype=np.int64)[None, :]
    phase = (t * f % length).astype(np.float64) * (2.0 * math.pi / length)
    cos, sin = np.cos(phase), -np.sin(phase)
    turn = t[:, 0] % 4
    sin[:, 0] = np.array([1.0, -1.0, -1.0, 1.0])[turn]
    forward = np.concatenate([cos, sin], axis=1)
    weight = np.full(2 * quarter, 2.0 / length)
    weight[0] = 1.0 / length
    inverse = (forward * weight).T
    return forward.astype(BF16), inverse.astype(BF16)


def dot(left, right):
    return jnp.dot(left, right, preferred_element_type=F32)


def one_hot(left, right):
    return (left == right).astype(F32).astype(BF16)


def iota(shape, axis):
    return lax.broadcasted_iota(jnp.int32, shape, axis)


def tile_at(j, tile=TILE):
    return slice(j * tile, (j + 1) * tile)


def start(source, target, sem):
    copy = pltpu.make_async_copy(source, target, sem)
    copy.start()
    return copy


def open_kernel(xlines, shots, source_hbm, target_hbm, mirror_hbm, live_hbm, rec_hbm, table_hbm, *refs):
    out_hbm, *parts_hbm = refs[: 1 + 2 * PARTS]
    lists_hbm = refs[1 + 2 * PARTS : 4 + 2 * PARTS]
    source_ref, target_ref, mirror_ref, live_ref, rec, table, spec, out, packed, *lists = refs[4 + 2 * PARTS : -4]
    index_sems, table_sems, out_sems, sems = refs[-4:]
    count, length = rec.shape
    quarter = length // 4
    indices = [
        start(source, target, index_sems.at[i])
        for i, (source, target) in enumerate(
            (
                (source_hbm, source_ref),
                (target_hbm, target_ref),
                (mirror_hbm, mirror_ref),
                (live_hbm, live_ref),
            )
        )
    ]
    first = start(rec_hbm, rec, sems.at[0])
    half = table.shape[0] // 2
    halves = [pl.ds(i * half, half) for i in range(2)]
    coming = [start(table_hbm.at[h], table.at[h], table_sems.at[i]) for i, h in enumerate(halves)]
    full_ref, fast_ref, put_ref = lists
    for copy in indices:
        copy.wait()

    me, line = lax.axis_index("shot"), lax.axis_index("xline")
    slots, owners = target_ref.shape
    entries = owners * slots
    spread = (lax.rem(iota((entries, slots), 0), slots) == iota((entries, slots), 1)).astype(F32)
    entry, owner = iota((entries, owners), 0), iota((entries, owners), 1)
    mine = (entry >= owner * slots) & (entry < (owner + 1) * slots)

    def column(values):
        wide = jnp.dot(spread, values.astype(F32), precision=lax.Precision.HIGHEST)
        return jnp.sum(jnp.where(mine, wide, 0.0), axis=1, keepdims=True).astype(jnp.int32)

    local = iota((1, count), 1)
    rx_local = count // shots
    live = iota((slots, owners), 0) < live_ref[...]
    target, mirrored = target_ref[...], mirror_ref[...]
    used_here = source_ref[pl.ds(pl.multiple_of(me * slots, slots), slots), :]
    dest = jnp.where(live, target * rx_local + lax.rem(used_here, rx_local), -1)
    offset = lax.rem(lax.div(mirrored, rx_local) + xlines - line, xlines)
    want = jnp.where(live, offset * count + target * rx_local + lax.rem(mirrored, rx_local), -1)
    send = jnp.sum(jnp.where(owner == me, source_ref[...], 0), axis=1, keepdims=True)
    give = one_hot(send, local)
    put_ref[...] = (column(dest) == local).astype(F32).T.astype(BF16)
    want = column(want)
    full_ref[...] = want

    named = (want == iota((1, xlines * count), 1)).astype(F32)
    counts = dot(jnp.ones((8, entries), BF16), named.astype(BF16))
    used = jnp.concatenate([counts[:1, tile_at(b, count)] for b in range(xlines)], axis=0) > 0.5
    used = used.astype(F32)
    earlier = (iota((count, count), 0) < iota((count, count), 1)).astype(F32).astype(BF16)
    rank = dot(used.astype(BF16), earlier)
    most = jnp.max(jnp.max(rank + used, axis=1, keepdims=True), axis=0, keepdims=True)
    over = (most > ROOM).astype(F32)
    places = jnp.concatenate([rank[b : b + 1] + float(b * ROOM) for b in range(xlines)], axis=1)
    place = jnp.sum(named * places, axis=1, keepdims=True).astype(jnp.int32)
    fast_ref[...] = jnp.where(want < 0, -1, place)
    pack = ((iota((ROOM, count), 0).astype(F32) == rank[:1]) & (used[:1] > 0.5)).astype(F32).astype(BF16)

    first.wait()
    odd = lax.rem(iota((1, length), 1), 2) == 1
    own = rec[...].astype(F32)
    both = jnp.concatenate([jnp.where(odd, 0.0, own), jnp.where(odd, own, 0.0)], axis=0).astype(BF16)
    for copy in coming:
        copy.wait()
    lane = iota((1, TILE), 1)
    for j in range(quarter // TILE):
        cos = dot(both, table[:, tile_at(j)])
        sin = dot(both, table[:, quarter + j * TILE : quarter + (j + 1) * TILE])
        cos_even, cos_odd, sin_even, sin_odd = cos[:count], cos[count:], sin[:count], sin[count:]
        parts = [cos_even + cos_odd, cos_even - cos_odd, sin_even + sin_odd, sin_odd - sin_even]
        if j == 0:
            parts[1] = jnp.where(lane == 0, sin_even, parts[1])
            parts[2] = jnp.where(lane == 0, 0.0, parts[2])
            parts[3] = jnp.where(lane == 0, sin_odd, parts[3])
        for p, part in enumerate(parts):
            spec[:, p * quarter + j * TILE : p * quarter + (j + 1) * TILE] = part.astype(BF16)
    for j in range(length // TILE):
        packed[:, tile_at(j)] = dot(pack, spec[:, tile_at(j)]).astype(BF16)
    going = [start(ref, hbm, index_sems.at[i]) for i, (ref, hbm) in enumerate(zip(lists, lists_hbm))]
    for p in range(PARTS):
        columns = tile_at(p, length // PARTS)
        going.append(start(packed.at[:, columns], parts_hbm[p], sems.at[1 + p]))
        going.append(start(spec.at[:, columns], parts_hbm[PARTS + p], sems.at[1 + PARTS + p]))
    for j in range(length // TILE):
        rows = dot(give, spec[:, tile_at(j)])
        if j * TILE == 2 * quarter:
            rows = jnp.where(lane == 0, over, rows)
        out[j] = rows.astype(BF16)
        going.append(start(out.at[j], out_hbm.at[:, tile_at(j)], out_sems.at[j]))
    for copy in going:
        copy.wait()


def open_rows(source, target, mirror, live, records, table, xlines, shots):
    count, length = records.shape
    entries = source.shape[0]
    steps = length // TILE
    lists = [
        jax.ShapeDtypeStruct((entries, 1), jnp.int32),
        jax.ShapeDtypeStruct((entries, 1), jnp.int32),
        jax.ShapeDtypeStruct((count, entries), BF16),
    ]
    return pl.pallas_call(
        functools.partial(open_kernel, xlines, shots),
        in_specs=[ANY] * 6,
        out_specs=[ANY] * (1 + 2 * PARTS + len(lists)),
        out_shape=[
            jax.ShapeDtypeStruct((entries, length), BF16),
            *[jax.ShapeDtypeStruct((ROOM, length // PARTS), BF16)] * PARTS,
            *[jax.ShapeDtypeStruct((count, length // PARTS), BF16)] * PARTS,
            *lists,
        ],
        scratch_shapes=[
            pltpu.VMEM(source.shape, jnp.int32),
            pltpu.VMEM(target.shape, jnp.int32),
            pltpu.VMEM(mirror.shape, jnp.int32),
            pltpu.VMEM(live.shape, jnp.int32),
            pltpu.VMEM((count, length), BF16),
            pltpu.VMEM(table.shape, BF16),
            pltpu.VMEM((count, length), BF16),
            pltpu.VMEM((steps, entries, TILE), BF16),
            pltpu.VMEM((ROOM, length), BF16),
            *[pltpu.VMEM(l.shape, l.dtype) for l in lists],
            pltpu.SemaphoreType.DMA((4,)),
            pltpu.SemaphoreType.DMA((2,)),
            pltpu.SemaphoreType.DMA((steps,)),
            pltpu.SemaphoreType.DMA((1 + 2 * PARTS,)),
        ],
        compiler_params=PARAMS,
    )(source, target, mirror, live, records, table)


def close_kernel(want_hbm, put_hbm, inverse_hbm, received_hbm, *refs):
    *chunks, out_ref, want_ref, put_ref, rows, received, inverse, rows_sems, sems = refs
    length = inverse.shape[1]
    quarter = length // 4
    size, columns = chunks[0].shape
    lists = [start(want_hbm, want_ref, sems.at[0]), start(put_hbm, put_ref, sems.at[1])]
    coming = []
    for i, chunk in enumerate(chunks):
        block, part = i // PARTS, i % PARTS
        place = rows.at[block * size : (block + 1) * size, part * columns : (part + 1) * columns]
        coming.append(start(chunk, place, rows_sems.at[i]))
    other = start(received_hbm, received, sems.at[2])
    table = start(inverse_hbm, inverse, sems.at[3])
    for copy in lists:
        copy.wait()
    take = one_hot(want_ref[...], iota((1, rows.shape[0]), 1))
    for copy in coming:
        copy.wait()
    put = put_ref[...]
    count = put.shape[0]
    lane = iota((1, TILE), 1)
    other.wait()
    stacks = []
    for j in range(quarter // TILE):
        sums = []
        for mirror in range(2):
            at = mirror * quarter + j * TILE
            re, im = slice(at, at + TILE), slice(2 * quarter + at, 2 * quarter + at + TILE)
            a_re, a_im = dot(take, rows[:, re]), dot(take, rows[:, im])
            b_re, b_im = received[:, re].astype(F32), received[:, im].astype(F32)
            for product in (a_re * b_re - a_im * b_im, a_re * b_im + a_im * b_re):
                high = product.astype(BF16)
                sums.append(dot(put, high).astype(BF16).astype(F32))
        re, im, mirror_re, mirror_im = sums
        even_re, odd_re, even_im, odd_im = re + mirror_re, re - mirror_re, im - mirror_im, im + mirror_im
        if j == 0:
            even_re, odd_re = jnp.where(lane == 0, re, even_re), jnp.where(lane == 0, re, odd_re)
            even_im, odd_im = jnp.where(lane == 0, mirror_re, even_im), jnp.where(lane == 0, mirror_im, odd_im)
        stacks.append(
            [jnp.concatenate(pair, axis=0).astype(BF16) for pair in ((even_re, odd_re), (even_im, odd_im))]
        )
    table.wait()
    odd = lax.rem(iota((1, TILE), 1), 2) == 1
    for c in range(length // TILE):
        acc = None
        for j, pair in enumerate(stacks):
            for p, stack in enumerate(pair):
                at = p * quarter + j * TILE
                part = dot(stack, inverse[at : at + TILE, tile_at(c)])
                acc = part if acc is None else acc + part
        out_ref[:, tile_at(c)] = jnp.where(odd, acc[count:], acc[:count])


def close(want, put, inverse, received, chunks):
    entries, length = received.shape
    return pl.pallas_call(
        close_kernel,
        in_specs=[ANY] * (4 + len(chunks)),
        out_specs=VMEM,
        out_shape=jax.ShapeDtypeStruct((put.shape[0], length), F32),
        scratch_shapes=[
            pltpu.VMEM(want.shape, jnp.int32),
            pltpu.VMEM(put.shape, BF16),
            pltpu.VMEM((len(chunks) // PARTS * chunks[0].shape[0], length), BF16),
            pltpu.VMEM((entries, length), BF16),
            pltpu.VMEM(inverse.shape, BF16),
            pltpu.SemaphoreType.DMA((len(chunks),)),
            pltpu.SemaphoreType.DMA((4,)),
        ],
        compiler_params=PARAMS,
    )(want, put, inverse, received, *chunks)


def ring(parts, xlines):
    up = [(i, (i + 1) % xlines) for i in range(xlines)]
    down = [(i, (i - 1) % xlines) for i in range(xlines)]
    half = xlines // 2
    below, above = list(parts), list(parts)
    chunks = {(0, s): part for s, part in enumerate(parts)}
    for step in range(1, half + 1):
        for s in range(2):
            if step < half or s == 1:
                above[s] = chunks[step, s] = lax.ppermute(above[s], "xline", down)
            if step < half or s == 0:
                below[s] = chunks[xlines - step, s] = lax.ppermute(below[s], "xline", up)
    return [chunks[o, s] for o in range(xlines) for s in range(2)]


def on_device(forward, inverse, records, source_trace, target_trace, mirror, live_slots):
    shot_dev, rx_local, length = records.shape
    count = shot_dev * rx_local
    xlines = lax.axis_size("xline")
    owners, _, slots = source_trace.shape
    source = source_trace.transpose(0, 2, 1).reshape(owners * slots, owners)
    outgoing, *parts, full, fast, put = open_rows(
        source,
        target_trace[0].T,
        mirror[0].T,
        live_slots,
        records.reshape(count, length),
        forward,
        xlines,
        shot_dev,
    )
    received = lax.all_to_all(
        outgoing.reshape(owners, slots, length), "shot", split_axis=0, concat_axis=0, tiled=True
    ).reshape(owners * slots, length)
    chunks = ring(parts[:PARTS], xlines)
    over = jnp.any(received[::slots, length // 2] != 0)

    def whole(received, spectra, full, fast, put, chunks):
        return close(full, put, inverse, received, ring(spectra, xlines))

    def short(received, spectra, full, fast, put, chunks):
        return close(fast, put, inverse, received, chunks)

    predicted = lax.cond(over, whole, short, received, parts[PARTS:], full, fast, put, chunks)
    return predicted.reshape(shot_dev, rx_local, length)


def solution(mesh):
    placed = (
        P("shot", "xline", None),
        P(),
        P("shot", None, None),
        P("shot", None, None),
        P("shot", None),
    )

    def run(*args):
        forward, inverse = tables(args[0].shape[-1])
        return jax.shard_map(
            on_device,
            mesh=mesh,
            in_specs=(P(), P(), *placed),
            out_specs=P("shot", "xline", None),
            check_vma=False,
        )(jnp.asarray(forward), jnp.asarray(inverse), *args)

    return run
```
